128 devices in a mesh: row: 8 (over x, z_hi), col: 16 (over y, z_lo, core).
Axes of the slice: x: 4, y: 4, z: 4 (z_hi: 2, z_lo: 2; z = z_hi * 2 + z_lo), core: 2. Of those that a mesh axis runs over, the one named last changes fastest.
Arguments:
- amplitude: float32 [32, 80, 5, 640], P('col', 'row'), may hold values from -6 to 6
- coupling: float32 [80, 5, 32, 640], P('row', None, 'col'), may hold values from -0.3125 to 0.3125
Outputs:
- cycle_term: float32 [32, 640, 32, 640], P('row', None, 'col')
The draws below stay inside these ranges and needn't reach their ends.
All inputs are finite; a program needn't handle non-finite values.
Results may differ from the reference program's by a relative error of at most 0.00005.
Values sent between devices are 32-bit elements; how exact they have to be, the bound alone decides.
No kernel may reach another device: no remote copies, remote signals or barrier semaphores. Data moves between devices by JAX's collectives and lax.ppermute only.
A program may use at most 128 MiB of HBM per device.

```python
import jax
import jax.numpy as jnp
from jax import lax

O = 80
V = 640
CB = 5
OW = 32


def levels(own_key, shape, split, low, high):
    def one(dim, blocks):
        steps = jax.random.uniform(jax.random.fold_in(jax.random.fold_in(own_key, 6), dim), (blocks,), jnp.float32, low / len(split), high / len(split))
        return jnp.repeat(jnp.exp(steps), shape[dim] // blocks).reshape((-1,) + (1,) * (len(shape) - dim - 1))

    factor_of = one(*split[0])
    for cut in split[1:]:
        factor_of = factor_of * one(*cut)
    return factor_of


def bell_draw(own_key, shape, width, bound, split=(), kind=jnp.bfloat16):
    level = levels(own_key, shape, split, -0.22, 0.18) if split else 1.0
    values = jax.random.normal(own_key, shape, jnp.float32) * width * level
    return jnp.minimum(jnp.maximum(values, -bound), bound).astype(kind)


def setup_inputs(seed: int = 0) -> dict:
    key_list = jax.random.split(jax.random.key(seed), 3)
    amplitude = bell_draw(key_list[0], (OW, O, CB, V), 1.0, 6.0, ((0, 16), (1, 8)), jnp.float32)
    coupling = bell_draw(key_list[1], (O, CB, OW, V), (O * CB) ** -0.5, 0.3125, ((0, 8), (2, 16)), jnp.float32)
    return dict(amplitude=amplitude, coupling=coupling)


def reference(amplitude, coupling):
    def one_row(index):
        own = lax.dynamic_index_in_dim(amplitude, index, 0, keepdims=False)
        side = lax.dynamic_index_in_dim(coupling, index, 2, keepdims=False)
        direct = jnp.einsum("kca,kcjb->ajb", own, coupling, precision=lax.Precision.HIGHEST)
        mirror = jnp.einsum("jkcb,kca->ajb", amplitude, side, precision=lax.Precision.HIGHEST)
        return direct + mirror

    return lax.map(one_row, jnp.arange(OW, dtype=jnp.int32))
```

```python
import functools

import jax
import jax.numpy as jnp
from jax import lax
from jax.experimental import pallas as pl
from jax.experimental.pallas import tpu as pltpu
from jax.sharding import PartitionSpec as P

AXES = ("row", "col")
BLOCK = 100
PARTS = 8
DEPTH = 800
MAIN = 768
REST = DEPTH - MAIN
WIDTH = 640
LANES = 128
CUTS = WIDTH // LANES


def flat(x, z, y, low, core):
    return ((x % 4) * 2 + z % 2) * 16 + ((y % 4) * 2 + low % 2) * 2 + core % 2


def permute(value, move):
    pairs = []
    for x in range(4):
        for z in range(2):
            for y in range(4):
                for low in range(2):
                    for core in range(2):
                        pairs.append((flat(x, z, y, low, core), flat(*move(x, z, y, low, core))))
    return lax.ppermute(value, AXES, pairs)


def split(value):
    high = value.astype(jnp.bfloat16)
    return high, (value - high.astype(jnp.float32)).astype(jnp.bfloat16)


def contract(*refs):
    js, own, other = refs[:8], refs[8:16], refs[16:24]
    out = refs[24]
    right, left, rh, rl, rr, lh, ll, lr, stage, sems, osems = refs[25:]
    row, col = lax.axis_index("row"), lax.axis_index("col")
    x, z = row // 2, row % 2
    y, low, core = col // 4, (col // 2) % 2, col % 2

    def place(a, b):
        return (((a + 8) % 4) * 2 + (b + 2) % 2) * BLOCK

    def slots(a, b):
        return [place(a, b), place(a, b + 1), place(a - 1, b), place(a + 1, b),
                place(a - 1, b + 1), place(a + 1, b + 1), place(a + 2, b), place(a + 2, b + 1)]

    def load(ref, cut, target, sem):
        return pltpu.make_async_copy(ref.at[:, :, pl.ds(cut * LANES, LANES)], target, sem)

    copies = []
    for cut in range(CUTS):
        for n, (ref, at) in enumerate(zip(js, slots(x, z))):
            copies.append(load(ref, cut, right.at[cut, pl.ds(at, BLOCK)], sems.at[cut, n]))
        for n, (ref, at) in enumerate(zip(own, slots(y, low))):
            copies.append(load(ref, cut, left.at[core, cut, pl.ds(at, BLOCK)], sems.at[cut, 8 + n]))
        for n, (ref, at) in enumerate(zip(other, slots(y, low))):
            copies.append(load(ref, cut, left.at[1 - core, cut, pl.ds(at, BLOCK)], sems.at[cut, 16 + n]))
    for copy in copies:
        copy.start()
    for copy in copies:
        copy.wait()

    right = right.reshape(CUTS, 2 * DEPTH, LANES)
    left = left.reshape(2, CUTS, 2 * DEPTH, LANES)
    flat_stage = stage.reshape(2, CUTS, 2 * WIDTH, LANES)

    for cut in range(CUTS):
        for j in range(2):
            cols = pl.ds((cut * 2 + j) * LANES, LANES)
            for k in range(0, MAIN, LANES):
                high, rest = split(right[cut, pl.ds(k * 2 + j, LANES, stride=2), :])
                rh[pl.ds(k, LANES), cols] = high
                rl[pl.ds(k, LANES), cols] = rest
            high, rest = split(right[cut, pl.ds(MAIN * 2 + j, REST, stride=2), :])
            rr[pl.ds(0, REST), cols] = high
            rr[pl.ds(REST, REST), cols] = rest
            rr[pl.ds(2 * REST, REST), cols] = high
            rr[pl.ds(3 * REST, REST), cols] = jnp.zeros_like(high)

    def turn(i, cut):
        half, j = i // 2, i % 2
        rows = pl.ds(pl.multiple_of(cut * LANES, LANES), LANES)
        for k in range(0, MAIN, LANES):
            high, rest = split(left[half, cut, pl.ds(k * 2 + j, LANES, stride=2), :].T)
            lh[rows, pl.ds(k, LANES)] = high
            ll[rows, pl.ds(k, LANES)] = rest
        value = left[half, cut, pl.ds(MAIN * 2 + j, REST, stride=2), :]
        high = value.astype(jnp.bfloat16).astype(jnp.float32)
        stack = jnp.concatenate([high, high, value - high, jnp.zeros_like(value)], axis=0)
        lr[rows, :] = stack.T.astype(jnp.bfloat16)

    def dot(a, b):
        return jnp.dot(a, b, preferred_element_type=jnp.float32)

    def flush(i, slot, cut):
        return pltpu.make_async_copy(
            stage.at[slot, cut], out.at[i, :, :, pl.ds(cut * LANES, LANES)], osems.at[slot, cut]
        )

    def one(i, carry):
        slot = i % 2

        def turn_one(cut, c):
            turn(i, cut)
            return c

        lax.fori_loop(0, CUTS, turn_one, 0)

        @pl.when(i >= 2)
        def _():
            for cut in range(CUTS):
                flush(i - 2, slot, cut).wait()

        def columns(cut, c):
            cols = pl.ds(pl.multiple_of(cut * 256, 256), 256)
            acc = dot(lh[...], rh[:, cols])
            acc += dot(lh[...], rl[:, cols])
            acc += dot(ll[...], rh[:, cols])
            acc += dot(lr[...], rr[:, cols])
            flat_stage[slot, cut, pl.ds(0, WIDTH, stride=2), :] = acc[:, :LANES]
            flat_stage[slot, cut, pl.ds(1, WIDTH, stride=2), :] = acc[:, LANES:]
            return c

        lax.fori_loop(0, CUTS, columns, 0)
        for cut in range(CUTS):
            flush(i, slot, cut).start()
        return carry

    lax.fori_loop(0, 4, one, 0)
    for i in (2, 3):
        for cut in range(CUTS):
            flush(i, i % 2, cut).wait()


def multiply(pieces):
    flops = 2 * 2560 * 1280 * 2400
    return pl.pallas_call(
        contract,
        out_shape=jax.ShapeDtypeStruct((4, WIDTH, 2, WIDTH), jnp.float32),
        in_specs=[pl.BlockSpec(memory_space=pl.ANY)] * 24,
        out_specs=pl.BlockSpec(memory_space=pl.ANY),
        scratch_shapes=[
            pltpu.VMEM((CUTS, DEPTH, 2, LANES), jnp.float32),
            pltpu.VMEM((2, CUTS, DEPTH, 2, LANES), jnp.float32),
            pltpu.VMEM((MAIN, 1280), jnp.bfloat16),
            pltpu.VMEM((MAIN, 1280), jnp.bfloat16),
            pltpu.VMEM((LANES, 1280), jnp.bfloat16),
            pltpu.VMEM((WIDTH, MAIN), jnp.bfloat16),
            pltpu.VMEM((WIDTH, MAIN), jnp.bfloat16),
            pltpu.VMEM((WIDTH, LANES), jnp.bfloat16),
            pltpu.VMEM((2, CUTS, WIDTH, 2, LANES), jnp.float32),
            pltpu.SemaphoreType.DMA((CUTS, 24)),
            pltpu.SemaphoreType.DMA((2, CUTS)),
        ],
        compiler_params=pltpu.CompilerParams(vmem_limit_bytes=56 * 1024 * 1024),
        cost_estimate=pl.CostEstimate(flops=flops, bytes_accessed=26 * 10**6, transcendentals=0),
    )(*pieces)


def shards(amplitude, coupling):
    a = jnp.transpose(amplitude, (1, 2, 0, 3))
    lefts = jnp.concatenate([a, coupling], axis=0).reshape(BLOCK, 2, WIDTH)
    rights = jnp.concatenate([coupling, a], axis=0).reshape(BLOCK, 2, WIDTH)

    def gather(first, second, up, down):
        a = permute(first, up)
        b = permute(first, down)
        c = permute(second, up)
        d = permute(second, down)
        e = permute(a, up)
        f = permute(d, down)
        return [first, second, a, b, c, d, e, f]

    turned = permute(lefts, lambda x, z, y, low, core: (y, low, x, z, core))
    far = permute(rights, lambda x, z, y, low, core: (x, z + 1, y, low, core))
    js = gather(rights, far,
                lambda x, z, y, low, core: (x + 1, z, y, low, core),
                lambda x, z, y, low, core: (x - 1, z, y, low, core))
    near = permute(turned, lambda x, z, y, low, core: (x, z, y, low + 1, core))
    own = gather(turned, near,
                 lambda x, z, y, low, core: (x, z, y + 1, low, core),
                 lambda x, z, y, low, core: (x, z, y - 1, low, core))
    other = [permute(v, lambda x, z, y, low, core: (x, z, y, low, core + 1)) for v in own]
    return multiply(js + own + other)


def solution(mesh):
    placed = (P("col", "row", None, None), P("row", None, "col", None))
    return jax.shard_map(
        shards, mesh=mesh, in_specs=placed, out_specs=P("row", None, "col", None), check_vma=False
    )
```

```python
import functools

import jax
import jax.numpy as jnp
from jax import lax
from jax.experimental import pallas as pl
from jax.experimental.pallas import tpu as pltpu
from jax.sharding import PartitionSpec as P

AXES = ("row", "col")
HALF = 50
GROUP = 4
PARTIAL = 2 * GROUP * HALF
MAIN = PARTIAL // 128 * 128
REST = PARTIAL - MAIN
DEPTH = 3 * MAIN + 128
WIDTH = 640
LANES = 128
CUTS = WIDTH // LANES
LIMIT = 40 * 1024 * 1024


def flat(x, z, y, low, core):
    return ((x % 4) * 2 + z % 2) * 16 + ((y % 4) * 2 + low % 2) * 2 + core % 2


def permute(value, move):
    pairs = []
    for x in range(4):
        for z in range(2):
            for y in range(4):
                for low in range(2):
                    for core in range(2):
                        pairs.append((flat(x, z, y, low, core), flat(*move(x, z, y, low, core))))
    return lax.ppermute(value, AXES, pairs)


def together(*values):
    return lax.optimization_barrier(values)


def split(value):
    high = value.astype(jnp.bfloat16)
    return high, (value - high.astype(jnp.float32)).astype(jnp.bfloat16)


def dot(a, b):
    return jnp.dot(a, b, preferred_element_type=jnp.float32)


def fetch(ref, half, target, at, cut, sem):
    return pltpu.make_async_copy(
        ref.at[pl.ds(half * HALF, HALF), :, pl.ds(cut * LANES, LANES)],
        target.at[cut, pl.ds(at, HALF)],
        sem,
    )


def fetch_lefts(refs, target, sems):
    copies = []
    for cut in range(CUTS):
        for half in range(2):
            for n, ref in enumerate(refs):
                at = half * GROUP * HALF + n * HALF
                copies.append(fetch(ref, half, target, at, cut, sems.at[cut, half, n]))
    return copies


def fill_right(source, first, target):
    for cut in range(CUTS):
        for j in range(2):
            cols = pl.ds((cut * 2 + j) * LANES, LANES)
            for k in range(0, MAIN, LANES):
                high, rest = split(source[cut, pl.ds((first + k) * 2 + j, LANES, stride=2), :])
                target[pl.ds(k, LANES), cols] = high
                target[pl.ds(MAIN + k, LANES), cols] = rest
                target[pl.ds(2 * MAIN + k, LANES), cols] = high
            high, rest = split(source[cut, pl.ds((first + MAIN) * 2 + j, REST, stride=2), :])
            target[pl.ds(3 * MAIN, REST), cols] = high
            target[pl.ds(3 * MAIN + REST, REST), cols] = rest
            target[pl.ds(3 * MAIN + 2 * REST, REST), cols] = high
            target[pl.ds(3 * MAIN + 3 * REST, 128 - 3 * REST), cols] = jnp.zeros((128 - 3 * REST, LANES), jnp.bfloat16)


def fill_left(source, j, cut, target):
    rows = pl.ds(cut * LANES, LANES)
    for k in range(0, MAIN, LANES):
        high, rest = split(source[cut, pl.ds(k * 2 + j, LANES, stride=2), :].T)
        target[rows, pl.ds(k, LANES)] = high
        target[rows, pl.ds(MAIN + k, LANES)] = high
        target[rows, pl.ds(2 * MAIN + k, LANES)] = rest
    value = source[cut, pl.ds(MAIN * 2 + j, REST, stride=2), :]
    high = value.astype(jnp.bfloat16).astype(jnp.float32)
    pad = jnp.zeros((128 - 3 * REST, LANES), jnp.float32)
    stack = jnp.concatenate([high, high, value - high, pad], axis=0)
    target[rows, pl.ds(3 * MAIN, LANES)] = stack.T.astype(jnp.bfloat16)


def fill_all(source, j, target):
    for cut in range(CUTS):
        fill_left(source, j, cut, target)


def begin(*refs):
    js, mine, theirs = refs[:8], refs[8:12], refs[12:14]
    total, later = refs[14:16]
    right, left, now, even, odd, jsems, isems = refs[16:]
    held = (even, odd)
    row, col = lax.axis_index("row"), lax.axis_index("col")
    x, z = row // 2, row % 2
    y, low, core = col // 4, (col // 2) % 2, col % 2
    way = 1 - 2 * core

    places = [(x, z), (x, z + 1), (x - way, z), (x + way, z),
              (x - way, z + 1), (x + way, z + 1), (x + 2, z), (x + 2, z + 1)]

    def position(a, b, half):
        delta = (a - (y - x + 2 * half) + 16) % 4
        other = (b + low + half) % 2
        side = jnp.where(delta == (4 - way) % 4, 2, 3) + 2 * other
        n = jnp.where(delta == 0, other, jnp.where(delta == 2, 6 + other, side))
        return (n // GROUP) * PARTIAL + half * GROUP * HALF + (n % GROUP) * HALF

    rights = []
    for half in range(2):
        for n, (ref, (a, b)) in enumerate(zip(js, places)):
            at = position(a, b, half)
            for cut in range(CUTS):
                rights.append(fetch(ref, half, right, at, cut, jsems.at[cut, half, n]))
    pieces = [theirs[n // 2].at[pl.ds(n % 2 * 2 * HALF, 2 * HALF)] for n in (0, 1, 3, 2)]
    lefts = [fetch_lefts(mine, left.at[0], isems.at[0]), fetch_lefts(pieces, left.at[1], isems.at[1])]
    for copy in rights + lefts[0] + lefts[1]:
        copy.start()
    for copy in rights:
        copy.wait()
    right = right.reshape(CUTS, 4 * PARTIAL, LANES)
    sources = [left.at[h].reshape(CUTS, 2 * PARTIAL, LANES) for h in range(2)]
    fill_right(right, 0, now)
    fill_right(right, PARTIAL, later)
    for half in range(2):
        for copy in lefts[half]:
            copy.wait()
    fill_all(sources[0], 0, held[0])
    for i in range(4):
        total[i] = dot(held[i % 2][...], now[...])
        if i < 3:
            fill_all(sources[(i + 1) // 2], (i + 1) % 2, held[(i + 1) % 2])


def finish(*refs):
    mine, theirs, total, now = refs[:4], refs[4:8], refs[8], refs[9]
    out, left, even, odd, before, stage, isems, osems = refs[10:]
    held = (even, odd)
    core = lax.axis_index("col") % 2
    lefts = [fetch_lefts(mine, left.at[0], isems.at[0]), fetch_lefts(theirs, left.at[1], isems.at[1])]

    def flush(i, cut):
        return pltpu.make_async_copy(
            stage.at[i % 2, cut],
            out.at[2 * ((core + i // 2) % 2) + i % 2, :, :, pl.ds(cut * LANES, LANES)],
            osems.at[i % 2, cut],
        )

    for copy in lefts[0]:
        copy.start()
    for copy in lefts[1]:
        copy.start()
    sources = [left.at[h].reshape(CUTS, 2 * PARTIAL, LANES) for h in range(2)]
    flat_stage = stage.reshape(2, CUTS, 2 * WIDTH, LANES)
    def store(i):
        for cut in range(CUTS):
            for j in range(2):
                at = (cut * 2 + j) * LANES
                flat_stage[i % 2, cut, pl.ds(j, WIDTH, stride=2), :] = before[:, pl.ds(at, LANES)]

    for half in range(2):
        for copy in lefts[half]:
            copy.wait()
    fill_all(sources[0], 0, held[0])
    for i in range(4):
        before[...] = total[i] + dot(held[i % 2][...], now[...])
        if i < 3:
            fill_all(sources[(i + 1) // 2], (i + 1) % 2, held[(i + 1) % 2])
        if i >= 2:
            for cut in range(CUTS):
                flush(i - 2, cut).wait()
        store(i)
        for cut in range(CUTS):
            flush(i, cut).start()
    for i in (2, 3):
        for cut in range(CUTS):
            flush(i, cut).wait()


ANY = pl.BlockSpec(memory_space=pl.ANY)
NEAR = pl.BlockSpec(memory_space=pltpu.VMEM)
WIDE = 10 * LANES


def start_products(js, mine, theirs):
    return pl.pallas_call(
        begin,
        out_shape=(
            pltpu.VMEM((4, WIDTH, WIDE), jnp.float32),
            pltpu.VMEM((DEPTH, WIDE), jnp.bfloat16),
        ),
        in_specs=[ANY] * 14,
        out_specs=(NEAR, NEAR),
        scratch_shapes=[
            pltpu.VMEM((CUTS, 2 * PARTIAL, 2, LANES), jnp.float32),
            pltpu.VMEM((2, CUTS, PARTIAL, 2, LANES), jnp.float32),
            pltpu.VMEM((DEPTH, WIDE), jnp.bfloat16),
            pltpu.VMEM((WIDTH, DEPTH), jnp.bfloat16),
            pltpu.VMEM((WIDTH, DEPTH), jnp.bfloat16),
            pltpu.SemaphoreType.DMA((CUTS, 2, 8)),
            pltpu.SemaphoreType.DMA((2, CUTS, 2, GROUP)),
        ],
        compiler_params=pltpu.CompilerParams(vmem_limit_bytes=LIMIT),
        cost_estimate=pl.CostEstimate(flops=10**6, bytes_accessed=10**5, transcendentals=0),
    )(*js, *mine, *theirs)


def end_products(mine, theirs, total, kept):
    return pl.pallas_call(
        finish,
        out_shape=jax.ShapeDtypeStruct((4, WIDTH, 2, WIDTH), jnp.float32),
        in_specs=[ANY] * 8 + [NEAR] * 2,
        out_specs=ANY,
        scratch_shapes=[
            pltpu.VMEM((2, CUTS, PARTIAL, 2, LANES), jnp.float32),
            pltpu.VMEM((WIDTH, DEPTH), jnp.bfloat16),
            pltpu.VMEM((WIDTH, DEPTH), jnp.bfloat16),
            pltpu.VMEM((WIDTH, WIDE), jnp.float32),
            pltpu.VMEM((2, CUTS, WIDTH, 2, LANES), jnp.float32),
            pltpu.SemaphoreType.DMA((2, CUTS, 2, GROUP)),
            pltpu.SemaphoreType.DMA((2, CUTS)),
        ],
        compiler_params=pltpu.CompilerParams(vmem_limit_bytes=LIMIT),
        cost_estimate=pl.CostEstimate(flops=2 * 2560 * 1280 * DEPTH, bytes_accessed=34 * 10**6, transcendentals=0),
    )(
        *mine,
        *theirs,
        pltpu.with_memory_space_constraint(total, pltpu.VMEM),
        pltpu.with_memory_space_constraint(kept, pltpu.VMEM),
    )


def shards(amplitude, coupling):
    amps = jnp.transpose(amplitude, (1, 2, 0, 3)).reshape(HALF, 2, WIDTH)
    ints = coupling.reshape(HALF, 2, WIDTH)
    block = jnp.concatenate([ints, amps], axis=0)

    def way(core):
        return 1 - 2 * core

    def right(x, z, y, low, core):
        return x + way(core), z, y, low, core

    def left(x, z, y, low, core):
        return x - way(core), z, y, low, core

    def up(x, z, y, low, core):
        return x, z, y + way(core), low, core

    def down(x, z, y, low, core):
        return x, z, y - way(core), low, core

    def near(x, z, y, low, core):
        return x, z, y, low + 1, core

    def tilt(value, shift):
        return permute(value, lambda x, z, y, low, core: (x, z, y + x + shift, low, core))

    def mirror(value, shift):
        return permute(
            value, lambda x, z, y, low, core: (y - x - shift, low, y, z + shift // 2, core)
        )

    def swap(value):
        return permute(value, lambda x, z, y, low, core: (x, z, y, low, core + 1))

    ta = tilt(amps, 0)
    tw = tilt(ints, 2)
    ja = permute(block, right)
    jb = permute(block, left)
    far = permute(block, lambda x, z, y, low, core: (x, z + 1, y, low, core))
    ta, tw = together(ta, tw)
    ma = mirror(ta, 0)
    mw = mirror(tw, 2)

    ma, mw, far, ja, jb = together(ma, mw, far, ja, jb)
    held = jnp.concatenate([ma, mw], axis=0)
    a = permute(held, up)
    b = permute(held, down)
    beside = permute(held, near)
    jc = permute(far, right)
    jd = permute(far, left)

    held, beside, a, b, ja, jc, jd = together(held, beside, a, b, ja, jc, jd)
    e = permute(a, up)
    je = permute(ja, right)
    jf = permute(jd, left)
    early = [swap(jnp.concatenate([held, beside], axis=0)), swap(jnp.concatenate([a, b], axis=0))]
    e, beside, *early = together(e, beside, *early)
    f = permute(e, near)
    c = permute(beside, up)
    d = permute(beside, down)
    js = [block, far, ja, jb, jc, jd, je, jf]
    total, kept = start_products(js, [held, beside, a, b], early)
    c, d, e, f, total = together(c, d, e, f, total)
    c2, d2, e2, f2 = swap(c), swap(d), swap(e), swap(f)
    return end_products([c, d, e, f], [d2, c2, e2, f2], total, kept)


def solution(mesh):
    placed = (P("col", "row", None, None), P("row", None, "col", None))
    return jax.shard_map(
        shards, mesh=mesh, in_specs=placed, out_specs=P("row", None, "col", None), check_vma=False
    )
```

```python
import jax
import jax.numpy as jnp
from jax import lax
from jax.experimental import pallas as pl
from jax.experimental.pallas import tpu as pltpu
from jax.sharding import PartitionSpec as P

AXES = ("row", "col")
HALF = 50
GROUP = 4
PARTIAL = 2 * GROUP * HALF
MAIN = PARTIAL // 128 * 128
REST = PARTIAL - MAIN
DEPTH = 3 * MAIN + 128
WIDTH = 640
LANES = 128
CUTS = WIDTH // LANES


def flat(x, z, y, low, core):
    return ((x % 4) * 2 + z % 2) * 16 + ((y % 4) * 2 + low % 2) * 2 + core % 2


def permute(value, move):
    pairs = []
    for x in range(4):
        for z in range(2):
            for y in range(4):
                for low in range(2):
                    for core in range(2):
                        pairs.append((flat(x, z, y, low, core), flat(*move(x, z, y, low, core))))
    return lax.ppermute(value, AXES, pairs)


def together(*values):
    return lax.optimization_barrier(values)


def split(value):
    high = value.astype(jnp.bfloat16)
    return high, (value - high.astype(jnp.float32)).astype(jnp.bfloat16)


def dot(a, b):
    return jnp.dot(a, b, preferred_element_type=jnp.float32)


def fetch(ref, half, target, at, cut, sem):
    return pltpu.make_async_copy(
        ref.at[pl.ds(half * HALF, HALF), :, pl.ds(cut * LANES, LANES)],
        target.at[cut, pl.ds(at, HALF)],
        sem,
    )


def fetch_lefts(refs, target, sems):
    copies = []
    for cut in range(CUTS):
        for half in range(2):
            for n, ref in enumerate(refs):
                at = half * GROUP * HALF + n * HALF
                copies.append(fetch(ref, half, target, at, cut, sems.at[cut, half, n]))
    return copies


def fill_right(source, first, target):
    for cut in range(CUTS):
        for j in range(2):
            cols = pl.ds((cut * 2 + j) * LANES, LANES)
            for k in range(0, MAIN, LANES):
                high, rest = split(source[cut, pl.ds((first + k) * 2 + j, LANES, stride=2), :])
                target[pl.ds(k, LANES), cols] = high
                target[pl.ds(MAIN + k, LANES), cols] = rest
                target[pl.ds(2 * MAIN + k, LANES), cols] = high
            high, rest = split(source[cut, pl.ds((first + MAIN) * 2 + j, REST, stride=2), :])
            target[pl.ds(3 * MAIN, REST), cols] = high
            target[pl.ds(3 * MAIN + REST, REST), cols] = rest
            target[pl.ds(3 * MAIN + 2 * REST, REST), cols] = high
            target[pl.ds(3 * MAIN + 3 * REST, 128 - 3 * REST), cols] = jnp.zeros((128 - 3 * REST, LANES), jnp.bfloat16)


def fill_left(source, j, cut, target):
    rows = pl.ds(cut * LANES, LANES)
    for k in range(0, MAIN, LANES):
        high, rest = split(source[cut, pl.ds(k * 2 + j, LANES, stride=2), :].T)
        target[rows, pl.ds(k, LANES)] = high
        target[rows, pl.ds(MAIN + k, LANES)] = high
        target[rows, pl.ds(2 * MAIN + k, LANES)] = rest
    value = source[cut, pl.ds(MAIN * 2 + j, REST, stride=2), :]
    high = value.astype(jnp.bfloat16).astype(jnp.float32)
    pad = jnp.zeros((128 - 3 * REST, LANES), jnp.float32)
    stack = jnp.concatenate([high, high, value - high, pad], axis=0)
    target[rows, pl.ds(3 * MAIN, LANES)] = stack.T.astype(jnp.bfloat16)


def fill_all(source, j, target):
    for cut in range(CUTS):
        fill_left(source, j, cut, target)


def places(z, x, way):
    return [(x, z), (x, z + 1), (x - way, z), (x + way, z),
            (x - way, z + 1), (x + way, z + 1), (x + 2, z), (x + 2, z + 1)]


def fetch_rights(refs, chosen, target, sems):
    row, col = lax.axis_index("row"), lax.axis_index("col")
    x, z = row // 2, row % 2
    y, low, core = col // 4, (col // 2) % 2, col % 2
    way = 1 - 2 * core
    copies = []
    for half in range(2):
        for m, (ref, n) in enumerate(zip(refs, chosen)):
            a, b = places(z, x, way)[n]
            delta = (a - (y - x + 2 * half) + 16) % 4
            other = (b + low + half) % 2
            side = jnp.where(delta == (4 - way) % 4, 2, 3) + 2 * other
            n = jnp.where(delta == 0, other, jnp.where(delta == 2, 6 + other, side))
            at = (n // GROUP) * PARTIAL + half * GROUP * HALF + (n % GROUP) * HALF
            for cut in range(CUTS):
                copies.append(fetch(ref, half, target, at, cut, sems.at[cut, half, m]))
    return copies


def prepare(*refs):
    js, mine = refs[:6], refs[6:10]
    right, held = refs[10:12]
    left, jsems, isems = refs[12:]
    lefts = fetch_lefts(mine, left, isems)
    rights = fetch_rights(js, range(6), right, jsems)
    for copy in lefts + rights:
        copy.start()
    for copy in lefts:
        copy.wait()
    for i in range(2):
        fill_all(left.reshape(CUTS, 2 * PARTIAL, LANES), i, held.at[i])
    for copy in rights:
        copy.wait()


def begin(je, jf, _, held, total, now, later, right, jsems):
    rights = fetch_rights([je, jf], (6, 7), right, jsems)
    for copy in rights:
        copy.start()
    for copy in rights:
        copy.wait()
    source = right.reshape(CUTS, 4 * PARTIAL, LANES)
    fill_right(source, 0, now)
    for i in range(2):
        total[i] = dot(held[i], now[...])
    fill_right(source, PARTIAL, later)


def scatter(out, side, stages, sums, sems):
    base = 2 * ((lax.axis_index("col") % 2 + side) % 2)
    flat_stages = [s.reshape(CUTS, 2 * WIDTH, LANES) for s in stages]

    def flush(i, cut):
        return pltpu.make_async_copy(
            stages[i].at[cut], out.at[base + i, :, :, pl.ds(cut * LANES, LANES)], sems.at[i, cut]
        )

    def store(i, cut):
        for j in range(2):
            value = sums[i][:, pl.ds((cut * 2 + j) * LANES, LANES)]
            flat_stages[i][cut, pl.ds(j, WIDTH, stride=2), :] = value

    return flush, store


def end(fill, product, flush, store):
    fill(0)
    product(0)
    fill(1)
    product(1)
    for cut in range(CUTS):
        store(0, cut)
    for cut in range(CUTS):
        flush(0, cut).start()
    for cut in range(CUTS):
        store(1, cut)
        flush(1, cut).start()
    for i in range(2):
        for cut in range(CUTS):
            flush(i, cut).wait()


def finish_own(*refs):
    pieces, total, later = refs[:4], refs[4], refs[5]
    out, left, even, odd, sums, other_sums, stage, other_stage, isems, osems = refs[6:]
    held, sums, stages = (even, odd), (sums, other_sums), (stage, other_stage)
    flush, store = scatter(out, 0, stages, sums, osems)
    lefts = fetch_lefts(pieces, left, isems)
    for copy in lefts:
        copy.start()
    for copy in lefts:
        copy.wait()
    source = left.reshape(CUTS, 2 * PARTIAL, LANES)

    def fill(i):
        fill_all(source, i, held[i])

    def product(i):
        sums[i][...] = dot(held[i][...], later[...]) + total[i]

    end(fill, product, flush, store)


def finish_other(*refs):
    early, pieces, now, later = refs[:2], refs[2:6], refs[6], refs[7]
    out, left, even, odd, next_even, next_odd, sums, other_sums, stage, other_stage, isems, osems = refs[9:]
    held, late_held = (even, odd), (next_even, next_odd)
    sums, stages = (sums, other_sums), (stage, other_stage)
    flush, store = scatter(out, 1, stages, sums, osems)
    first = [early[n // 2].at[pl.ds(n % 2 * 2 * HALF, 2 * HALF)] for n in (0, 1, 3, 2)]
    lefts = [fetch_lefts(first, left.at[0], isems.at[0]), fetch_lefts(pieces, left.at[1], isems.at[1])]
    for copy in lefts[0] + lefts[1]:
        copy.start()
    for copy in lefts[0]:
        copy.wait()
    sources = [left.at[h].reshape(CUTS, 2 * PARTIAL, LANES) for h in range(2)]
    fill_all(sources[0], 0, held[0])
    for copy in lefts[1]:
        copy.wait()
    sums[0][...] = dot(held[0][...], now[...])
    fill_all(sources[1], 0, late_held[0])
    sums[0][...] += dot(late_held[0][...], later[...])
    fill_all(sources[0], 1, held[1])
    sums[1][...] = dot(held[1][...], now[...])
    fill_all(sources[1], 1, late_held[1])
    sums[1][...] += dot(late_held[1][...], later[...])
    for i in range(2):
        for cut in range(CUTS):
            store(i, cut)
            flush(i, cut).start()
    for i in range(2):
        for cut in range(CUTS):
            flush(i, cut).wait()


ANY = pl.BlockSpec(memory_space=pl.ANY)
NEAR = pl.BlockSpec(memory_space=pltpu.VMEM)
WIDE = 10 * LANES
HELD = pltpu.VMEM((WIDTH, DEPTH), jnp.bfloat16)
LEFT = pltpu.VMEM((CUTS, PARTIAL, 2, LANES), jnp.float32)
LEFT_SEMS = pltpu.SemaphoreType.DMA((CUTS, 2, GROUP))
PANEL = pltpu.VMEM((DEPTH, WIDE), jnp.bfloat16)
SUMS = pltpu.VMEM((2, WIDTH, WIDE), jnp.float32)
HELDS = pltpu.VMEM((2, WIDTH, DEPTH), jnp.bfloat16)
RIGHT = pltpu.VMEM((CUTS, 2 * PARTIAL, 2, LANES), jnp.float32)
SUM = pltpu.VMEM((WIDTH, WIDE), jnp.float32)
STAGE = pltpu.VMEM((CUTS, WIDTH, 2, LANES), jnp.float32)
LIMIT = 28 * 1024 * 1024
COST = pl.CostEstimate(flops=10**6, bytes_accessed=10**5, transcendentals=0)


def near(value):
    return pltpu.with_memory_space_constraint(value, pltpu.VMEM)


def call(kernel, args, kinds, shapes, scratch, aliases=None):
    nears = [near(arg) if kind is NEAR else arg for arg, kind in zip(args, kinds)]
    outs = [NEAR if isinstance(shape, type(SUMS)) else ANY for shape in shapes]
    return pl.pallas_call(
        kernel,
        out_shape=tuple(shapes),
        in_specs=kinds,
        out_specs=tuple(outs),
        scratch_shapes=scratch,
        input_output_aliases=aliases or {},
        compiler_params=pltpu.CompilerParams(vmem_limit_bytes=LIMIT),
        cost_estimate=COST,
    )(*nears)


def prepare_call(js, mine):
    scratch = [LEFT, pltpu.SemaphoreType.DMA((CUTS, 2, 6)), LEFT_SEMS]
    return call(prepare, [*js, *mine], [ANY] * 10, [RIGHT, HELDS], scratch)


def begin_call(js, right, held):
    scratch = [pltpu.SemaphoreType.DMA((CUTS, 2, 2))]
    args = [*js, right, held]
    return call(begin, args, [ANY] * 2 + [NEAR] * 2, [SUMS, PANEL, PANEL, RIGHT], scratch, {2: 3})[:3]


OUT = jax.ShapeDtypeStruct((4, WIDTH, 2, WIDTH), jnp.float32)
OUT_SEMS = pltpu.SemaphoreType.DMA((2, CUTS))


def own_call(pieces, total, later):
    scratch = [LEFT, HELD, HELD, SUM, SUM, STAGE, STAGE, LEFT_SEMS, OUT_SEMS]
    return call(finish_own, [*pieces, total, later], [ANY] * 4 + [NEAR] * 2, [OUT], scratch)[0]


def other_call(early, pieces, now, later, out):
    scratch = [
        pltpu.VMEM((2, CUTS, PARTIAL, 2, LANES), jnp.float32),
        HELD, HELD, HELD, HELD, SUM, SUM, STAGE, STAGE,
        pltpu.SemaphoreType.DMA((2, CUTS, 2, GROUP)),
        OUT_SEMS,
    ]
    args = [*early, *pieces, now, later, out]
    return call(finish_other, args, [ANY] * 6 + [NEAR] * 2 + [ANY], [OUT], scratch, {8: 0})[0]


def shards(amplitude, coupling):
    amps = jnp.transpose(amplitude, (1, 2, 0, 3)).reshape(HALF, 2, WIDTH)
    ints = coupling.reshape(HALF, 2, WIDTH)
    block = jnp.concatenate([ints, amps], axis=0)

    def way(core):
        return 1 - 2 * core

    def right(x, z, y, low, core):
        return x + way(core), z, y, low, core

    def left(x, z, y, low, core):
        return x - way(core), z, y, low, core

    def up(x, z, y, low, core):
        return x, z, y + way(core), low, core

    def down(x, z, y, low, core):
        return x, z, y - way(core), low, core

    def beyond(x, z, y, low, core):
        return x, z, y, low + 1, core

    def tilt(value, shift):
        return permute(value, lambda x, z, y, low, core: (x, z, y + x + shift, low, core))

    def mirror(value, shift):
        return permute(
            value, lambda x, z, y, low, core: (y - x - shift, low, y, z + shift // 2, core)
        )

    def swap(value):
        return permute(value, lambda x, z, y, low, core: (x, z, y, low, core + 1))

    amps, ints, block = together(amps, ints, block)
    far = permute(block, lambda x, z, y, low, core: (x, z + 1, y, low, core))
    ta = tilt(amps, 0)
    tw = tilt(ints, 2)
    ja = permute(block, right)
    jb = permute(block, left)
    ta, tw = together(ta, tw)
    ma = mirror(ta, 0)
    mw = mirror(tw, 2)

    ma, mw, ja, jb, far = together(ma, mw, ja, jb, far)
    held = jnp.concatenate([ma, mw], axis=0)
    a = permute(held, up)
    b = permute(held, down)
    beside = permute(held, beyond)
    jc = permute(far, right)
    jd = permute(far, left)
    e = permute(a, up)

    ja, jc, jd = together(ja, jc, jd)
    je = permute(ja, right)
    jf = permute(jd, left)
    e, beside = together(e, beside)
    f = permute(e, beyond)
    c = permute(beside, up)
    d = permute(beside, down)

    panel, helds = prepare_call([block, far, ja, jb, jc, jd], [held, beside, a, b])
    own, now, later = begin_call([je, jf], panel, helds)
    held, beside, a, b, e, c, d, f, own = together(held, beside, a, b, e, c, d, f, own)
    early = [swap(jnp.concatenate([held, beside], axis=0)), swap(jnp.concatenate([a, b], axis=0))]
    late = [swap(v) for v in (d, c, e, f)]
    out = own_call([c, d, e, f], own, later)
    return other_call(early, late, now, later, out)


def solution(mesh):
    placed = (P("col", "row", None, None), P("row", None, "col", None))
    return jax.shard_map(
        shards, mesh=mesh, in_specs=placed, out_specs=P("row", None, "col", None), check_vma=False
    )
```

```python
import jax
import jax.numpy as jnp
from jax import lax
from jax.experimental import pallas as pl
from jax.experimental.pallas import tpu as pltpu
from jax.sharding import PartitionSpec as P

AXES = ("row", "col")
HALF = 50
GROUP = 4
PARTIAL = 2 * GROUP * HALF
MAIN = PARTIAL // 128 * 128
REST = PARTIAL - MAIN
DEPTH = 3 * MAIN + 128
WIDTH = 640
LANES = 128
CUTS = WIDTH // LANES


def flat(x, z, y, low, core):
    return ((x % 4) * 2 + z % 2) * 16 + ((y % 4) * 2 + low % 2) * 2 + core % 2


def permute(value, move):
    pairs = []
    for x in range(4):
        for z in range(2):
            for y in range(4):
                for low in range(2):
                    for core in range(2):
                        pairs.append((flat(x, z, y, low, core), flat(*move(x, z, y, low, core))))
    return lax.ppermute(value, AXES, pairs)


def together(*values):
    return lax.optimization_barrier(values)


def split(value):
    high = value.astype(jnp.bfloat16)
    return high, (value - high.astype(jnp.float32)).astype(jnp.bfloat16)


def dot(a, b):
    return jnp.dot(a, b, preferred_element_type=jnp.float32)


def fetch(ref, half, target, at, cut, sem):
    return pltpu.make_async_copy(
        ref.at[pl.ds(half * HALF, HALF), :, pl.ds(cut * LANES, LANES)],
        target.at[cut, pl.ds(at, HALF)],
        sem,
    )


def fetch_lefts(refs, target, sems):
    copies = []
    for cut in range(CUTS):
        for half in range(2):
            for n, ref in enumerate(refs):
                at = half * GROUP * HALF + n * HALF
                copies.append(fetch(ref, half, target, at, cut, sems.at[cut, half, n]))
    return copies


def fill_right(source, first, target):
    for cut in range(CUTS):
        for j in range(2):
            cols = pl.ds((cut * 2 + j) * LANES, LANES)
            for k in range(0, MAIN, LANES):
                high, rest = split(source[cut, pl.ds((first + k) * 2 + j, LANES, stride=2), :])
                target[pl.ds(k, LANES), cols] = high
                target[pl.ds(MAIN + k, LANES), cols] = rest
                target[pl.ds(2 * MAIN + k, LANES), cols] = high
            high, rest = split(source[cut, pl.ds((first + MAIN) * 2 + j, REST, stride=2), :])
            target[pl.ds(3 * MAIN, REST), cols] = high
            target[pl.ds(3 * MAIN + REST, REST), cols] = rest
            target[pl.ds(3 * MAIN + 2 * REST, REST), cols] = high
            target[pl.ds(3 * MAIN + 3 * REST, 128 - 3 * REST), cols] = jnp.zeros((128 - 3 * REST, LANES), jnp.bfloat16)


def fill_left(source, j, cut, target):
    rows = pl.ds(cut * LANES, LANES)
    for k in range(0, MAIN, LANES):
        high, rest = split(source[cut, pl.ds(k * 2 + j, LANES, stride=2), :].T)
        target[rows, pl.ds(k, LANES)] = high
        target[rows, pl.ds(MAIN + k, LANES)] = high
        target[rows, pl.ds(2 * MAIN + k, LANES)] = rest
    value = source[cut, pl.ds(MAIN * 2 + j, REST, stride=2), :]
    high = value.astype(jnp.bfloat16).astype(jnp.float32)
    pad = jnp.zeros((128 - 3 * REST, LANES), jnp.float32)
    stack = jnp.concatenate([high, high, value - high, pad], axis=0)
    target[rows, pl.ds(3 * MAIN, LANES)] = stack.T.astype(jnp.bfloat16)


def fill_all(source, j, target):
    for cut in range(CUTS):
        fill_left(source, j, cut, target)


def places(z, x, way):
    return [(x, z), (x, z + 1), (x - way, z), (x + way, z),
            (x - way, z + 1), (x + way, z + 1), (x + 2, z), (x + 2, z + 1)]


def fetch_rights(refs, chosen, target, sems):
    row, col = lax.axis_index("row"), lax.axis_index("col")
    x, z = row // 2, row % 2
    y, low, core = col // 4, (col // 2) % 2, col % 2
    way = 1 - 2 * core
    copies = []
    for half in range(2):
        for m, (ref, n) in enumerate(zip(refs, chosen)):
            a, b = places(z, x, way)[n]
            delta = (a - (x - y + 2 * half) + 16) % 4
            other = (b + low + half) % 2
            side = jnp.where(delta == (4 + way) % 4, 2, 3) + 2 * other
            n = jnp.where(delta == 0, other, jnp.where(delta == 2, 6 + other, side))
            at = (n // GROUP) * PARTIAL + half * GROUP * HALF + (n % GROUP) * HALF
            for cut in range(CUTS):
                copies.append(fetch(ref, half, target, at, cut, sems.at[cut, half, m]))
    return copies


def prepare(*refs):
    js, mine = refs[:6], refs[6:10]
    right, held = refs[10:12]
    left, jsems, isems = refs[12:]
    lefts = fetch_lefts(mine, left, isems)
    rights = fetch_rights(js, range(6), right, jsems)
    for copy in lefts + rights:
        copy.start()
    for copy in lefts:
        copy.wait()
    for i in range(2):
        fill_all(left.reshape(CUTS, 2 * PARTIAL, LANES), i, held.at[i])
    for copy in rights:
        copy.wait()


def begin(je, jf, _, held, total, now, later, right, jsems):
    rights = fetch_rights([je, jf], (6, 7), right, jsems)
    for copy in rights:
        copy.start()
    for copy in rights:
        copy.wait()
    source = right.reshape(CUTS, 4 * PARTIAL, LANES)
    fill_right(source, 0, now)
    for i in range(2):
        total[i] = dot(held[i], now[...])
    fill_right(source, PARTIAL, later)


def scatter(out, side, stages, sums, sems):
    base = 2 * ((lax.axis_index("col") % 2 + side) % 2)
    flat_stages = [s.reshape(CUTS, 2 * WIDTH, LANES) for s in stages]

    def flush(i, cut):
        return pltpu.make_async_copy(
            stages[i].at[cut], out.at[base + i, :, :, pl.ds(cut * LANES, LANES)], sems.at[i, cut]
        )

    def store(i, cut):
        for j in range(2):
            value = sums[i][:, pl.ds((cut * 2 + j) * LANES, LANES)]
            flat_stages[i][cut, pl.ds(j, WIDTH, stride=2), :] = value

    return flush, store


def end(fill, product, flush, store):
    fill(0)
    product(0)
    fill(1)
    product(1)
    for cut in range(CUTS):
        store(0, cut)
    for cut in range(CUTS):
        flush(0, cut).start()
    for cut in range(CUTS):
        store(1, cut)
        flush(1, cut).start()
    for i in range(2):
        for cut in range(CUTS):
            flush(i, cut).wait()


def finish_own(*refs):
    pieces, total, later = refs[:4], refs[4], refs[5]
    out, left, even, odd, sums, other_sums, stage, other_stage, isems, osems = refs[6:]
    held, sums, stages = (even, odd), (sums, other_sums), (stage, other_stage)
    flush, store = scatter(out, 0, stages, sums, osems)
    lefts = fetch_lefts(pieces, left, isems)
    for copy in lefts:
        copy.start()
    for copy in lefts:
        copy.wait()
    source = left.reshape(CUTS, 2 * PARTIAL, LANES)

    def fill(i):
        fill_all(source, i, held[i])

    def product(i):
        sums[i][...] = dot(held[i][...], later[...]) + total[i]

    end(fill, product, flush, store)


def finish_other(*refs):
    early, pieces, now, later = refs[:2], refs[2:6], refs[6], refs[7]
    out, left, even, odd, next_even, next_odd, sums, other_sums, stage, other_stage, isems, osems = refs[9:]
    held, late_held = (even, odd), (next_even, next_odd)
    sums, stages = (sums, other_sums), (stage, other_stage)
    flush, store = scatter(out, 1, stages, sums, osems)
    first = [early[n // 2].at[pl.ds(n % 2 * 2 * HALF, 2 * HALF)] for n in (0, 1, 3, 2)]
    lefts = [fetch_lefts(first, left.at[0], isems.at[0]), fetch_lefts(pieces, left.at[1], isems.at[1])]
    for copy in lefts[0] + lefts[1]:
        copy.start()
    for copy in lefts[0]:
        copy.wait()
    sources = [left.at[h].reshape(CUTS, 2 * PARTIAL, LANES) for h in range(2)]
    fill_all(sources[0], 0, held[0])
    for copy in lefts[1]:
        copy.wait()
    sums[0][...] = dot(held[0][...], now[...])
    fill_all(sources[1], 0, late_held[0])
    sums[0][...] += dot(late_held[0][...], later[...])
    fill_all(sources[0], 1, held[1])
    sums[1][...] = dot(held[1][...], now[...])
    fill_all(sources[1], 1, late_held[1])
    sums[1][...] += dot(late_held[1][...], later[...])
    for i in range(2):
        for cut in range(CUTS):
            store(i, cut)
            flush(i, cut).start()
    for i in range(2):
        for cut in range(CUTS):
            flush(i, cut).wait()


ANY = pl.BlockSpec(memory_space=pl.ANY)
NEAR = pl.BlockSpec(memory_space=pltpu.VMEM)
WIDE = 10 * LANES
HELD = pltpu.VMEM((WIDTH, DEPTH), jnp.bfloat16)
LEFT = pltpu.VMEM((CUTS, PARTIAL, 2, LANES), jnp.float32)
LEFT_SEMS = pltpu.SemaphoreType.DMA((CUTS, 2, GROUP))
PANEL = pltpu.VMEM((DEPTH, WIDE), jnp.bfloat16)
SUMS = pltpu.VMEM((2, WIDTH, WIDE), jnp.float32)
HELDS = pltpu.VMEM((2, WIDTH, DEPTH), jnp.bfloat16)
RIGHT = pltpu.VMEM((CUTS, 2 * PARTIAL, 2, LANES), jnp.float32)
SUM = pltpu.VMEM((WIDTH, WIDE), jnp.float32)
STAGE = pltpu.VMEM((CUTS, WIDTH, 2, LANES), jnp.float32)
LIMIT = 28 * 1024 * 1024
COST = pl.CostEstimate(flops=10**6, bytes_accessed=10**5, transcendentals=0)


def near(value):
    return pltpu.with_memory_space_constraint(value, pltpu.VMEM)


def call(kernel, args, kinds, shapes, scratch, aliases=None):
    nears = [near(arg) if kind is NEAR else arg for arg, kind in zip(args, kinds)]
    outs = [NEAR if isinstance(shape, type(SUMS)) else ANY for shape in shapes]
    return pl.pallas_call(
        kernel,
        out_shape=tuple(shapes),
        in_specs=kinds,
        out_specs=tuple(outs),
        scratch_shapes=scratch,
        input_output_aliases=aliases or {},
        compiler_params=pltpu.CompilerParams(vmem_limit_bytes=LIMIT),
        cost_estimate=COST,
    )(*nears)


def prepare_call(js, mine):
    scratch = [LEFT, pltpu.SemaphoreType.DMA((CUTS, 2, 6)), LEFT_SEMS]
    return call(prepare, [*js, *mine], [ANY] * 10, [RIGHT, HELDS], scratch)


def begin_call(js, right, held):
    scratch = [pltpu.SemaphoreType.DMA((CUTS, 2, 2))]
    args = [*js, right, held]
    return call(begin, args, [ANY] * 2 + [NEAR] * 2, [SUMS, PANEL, PANEL, RIGHT], scratch, {2: 3})[:3]


OUT = jax.ShapeDtypeStruct((4, WIDTH, 2, WIDTH), jnp.float32)
OUT_SEMS = pltpu.SemaphoreType.DMA((2, CUTS))


def own_call(pieces, total, later):
    scratch = [LEFT, HELD, HELD, SUM, SUM, STAGE, STAGE, LEFT_SEMS, OUT_SEMS]
    return call(finish_own, [*pieces, total, later], [ANY] * 4 + [NEAR] * 2, [OUT], scratch)[0]


def other_call(early, pieces, now, later, out):
    scratch = [
        pltpu.VMEM((2, CUTS, PARTIAL, 2, LANES), jnp.float32),
        HELD, HELD, HELD, HELD, SUM, SUM, STAGE, STAGE,
        pltpu.SemaphoreType.DMA((2, CUTS, 2, GROUP)),
        OUT_SEMS,
    ]
    args = [*early, *pieces, now, later, out]
    return call(finish_other, args, [ANY] * 6 + [NEAR] * 2 + [ANY], [OUT], scratch, {8: 0})[0]


def shards(amplitude, coupling):
    amps = jnp.transpose(amplitude, (1, 2, 0, 3)).reshape(HALF, 2, WIDTH)
    ints = coupling.reshape(HALF, 2, WIDTH)
    block = jnp.concatenate([ints, amps], axis=0)

    def way(core):
        return 1 - 2 * core

    def right(x, z, y, low, core):
        return x + way(core), z, y, low, core

    def left(x, z, y, low, core):
        return x - way(core), z, y, low, core

    def up(x, z, y, low, core):
        return x, z, y + way(core), low, core

    def down(x, z, y, low, core):
        return x, z, y - way(core), low, core

    def beyond(x, z, y, low, core):
        return x, z, y, low + 1, core

    def tilt(value, shift):
        return permute(value, lambda x, z, y, low, core: (x, low, y - x + shift, z + shift // 2, core))

    def mirror(value, shift):
        return permute(
            value, lambda x, z, y, low, core: (y + x - shift, z, y, low, core)
        )

    def swap(value):
        return permute(value, lambda x, z, y, low, core: (x, z, y, low, core + 1))

    amps, ints, block = together(amps, ints, block)
    far = permute(block, lambda x, z, y, low, core: (x, z + 1, y, low, core))
    ta = tilt(amps, 0)
    tw = tilt(ints, 2)
    ja = permute(block, right)
    jb = permute(block, left)
    ta, tw = together(ta, tw)
    ma = mirror(ta, 0)
    mw = mirror(tw, 2)

    ma, mw, ja, jb, far = together(ma, mw, ja, jb, far)
    held = jnp.concatenate([ma, mw], axis=0)
    a = permute(held, up)
    b = permute(held, down)
    beside = permute(held, beyond)
    jc = permute(far, right)
    jd = permute(far, left)
    e = permute(a, up)

    ja, jc, jd = together(ja, jc, jd)
    je = permute(ja, right)
    jf = permute(jd, left)
    e, beside = together(e, beside)
    f = permute(e, beyond)
    c = permute(beside, up)
    d = permute(beside, down)

    panel, helds = prepare_call([block, far, ja, jb, jc, jd], [held, beside, a, b])
    own, now, later = begin_call([je, jf], panel, helds)
    held, beside, a, b, e, c, d, f, own = together(held, beside, a, b, e, c, d, f, own)
    early = [swap(jnp.concatenate([held, beside], axis=0)), swap(jnp.concatenate([a, b], axis=0))]
    late = [swap(v) for v in (d, c, e, f)]
    out = own_call([c, d, e, f], own, later)
    return other_call(early, late, now, later, out)


def solution(mesh):
    placed = (P("col", "row", None, None), P("row", None, "col", None))
    return jax.shard_map(
        shards, mesh=mesh, in_specs=placed, out_specs=P("row", None, "col", None), check_vma=False
    )
```

```python
import jax
import jax.numpy as jnp
from jax import lax
from jax.experimental import pallas as pl
from jax.experimental.pallas import tpu as pltpu
from jax.sharding import PartitionSpec as P

AXES = ("row", "col")
HALF = 50
GROUP = 4
PARTIAL = 2 * GROUP * HALF
MAIN = PARTIAL // 128 * 128
REST = PARTIAL - MAIN
DEPTH = 3 * MAIN + 128
WIDTH = 640
LANES = 128
CUTS = WIDTH // LANES


def flat(x, z, y, low, core):
    return ((x % 4) * 2 + z % 2) * 16 + ((y % 4) * 2 + low % 2) * 2 + core % 2


def permute(value, move):
    pairs = []
    for x in range(4):
        for z in range(2):
            for y in range(4):
                for low in range(2):
                    for core in range(2):
                        pairs.append((flat(x, z, y, low, core), flat(*move(x, z, y, low, core))))
    return lax.ppermute(value, AXES, pairs)


def together(*values):
    return lax.optimization_barrier(values)


def split(value):
    high = value.astype(jnp.bfloat16)
    return high, (value - high.astype(jnp.float32)).astype(jnp.bfloat16)


def dot(a, b):
    return jnp.dot(a, b, preferred_element_type=jnp.float32)


def fetch(ref, half, target, at, cut, sem):
    return pltpu.make_async_copy(
        ref.at[pl.ds(half * HALF, HALF), :, pl.ds(cut * LANES, LANES)],
        target.at[cut, pl.ds(at, HALF)],
        sem,
    )


def fetch_lefts(refs, target, sems):
    copies = []
    for cut in range(CUTS):
        for half in range(2):
            for n, ref in enumerate(refs):
                at = half * GROUP * HALF + n * HALF
                copies.append(fetch(ref, half, target, at, cut, sems.at[cut, half, n]))
    return copies


def fill_right(source, first, target):
    for cut in range(CUTS):
        for j in range(2):
            cols = pl.ds((cut * 2 + j) * LANES, LANES)
            for k in range(0, MAIN, LANES):
                high, rest = split(source[cut, pl.ds((first + k) * 2 + j, LANES, stride=2), :])
                target[pl.ds(k, LANES), cols] = high
                target[pl.ds(MAIN + k, LANES), cols] = rest
                target[pl.ds(2 * MAIN + k, LANES), cols] = high
            high, rest = split(source[cut, pl.ds((first + MAIN) * 2 + j, REST, stride=2), :])
            target[pl.ds(3 * MAIN, REST), cols] = high
            target[pl.ds(3 * MAIN + REST, REST), cols] = rest
            target[pl.ds(3 * MAIN + 2 * REST, REST), cols] = high
            target[pl.ds(3 * MAIN + 3 * REST, 128 - 3 * REST), cols] = jnp.zeros((128 - 3 * REST, LANES), jnp.bfloat16)


def fill_left(source, j, cut, target):
    rows = pl.ds(cut * LANES, LANES)
    for k in range(0, MAIN, LANES):
        high, rest = split(source[cut, pl.ds(k * 2 + j, LANES, stride=2), :].T)
        target[rows, pl.ds(k, LANES)] = high
        target[rows, pl.ds(MAIN + k, LANES)] = high
        target[rows, pl.ds(2 * MAIN + k, LANES)] = rest
    value = source[cut, pl.ds(MAIN * 2 + j, REST, stride=2), :]
    high = value.astype(jnp.bfloat16).astype(jnp.float32)
    pad = jnp.zeros((128 - 3 * REST, LANES), jnp.float32)
    stack = jnp.concatenate([high, high, value - high, pad], axis=0)
    target[rows, pl.ds(3 * MAIN, LANES)] = stack.T.astype(jnp.bfloat16)


def fill_all(source, j, target):
    for cut in range(CUTS):
        fill_left(source, j, cut, target)


def places(z, x, way):
    return [(x, z), (x, z + 1), (x - way, z), (x + way, z),
            (x - way, z + 1), (x + way, z + 1), (x + 2, z), (x + 2, z + 1)]


def fetch_rights(refs, chosen, target, sems):
    row, col = lax.axis_index("row"), lax.axis_index("col")
    x, z = row // 2, row % 2
    y, low, core = col // 4, (col // 2) % 2, col % 2
    way = 1 - 2 * core
    copies = []
    for half in range(2):
        for m, (ref, n) in enumerate(zip(refs, chosen)):
            a, b = places(z, x, way)[n]
            delta = (a - (x - y + 2 * half) + 16) % 4
            other = (b + low + half) % 2
            side = jnp.where(delta == (4 + way) % 4, 2, 3) + 2 * other
            n = jnp.where(delta == 0, other, jnp.where(delta == 2, 6 + other, side))
            at = (n // GROUP) * PARTIAL + half * GROUP * HALF + (n % GROUP) * HALF
            for cut in range(CUTS):
                copies.append(fetch(ref, half, target, at, cut, sems.at[cut, half, m]))
    return copies


def prepare(*refs):
    js, mine = refs[:6], refs[6:10]
    right, held = refs[10:12]
    left, jsems, isems = refs[12:]
    lefts = fetch_lefts(mine, left, isems)
    rights = fetch_rights(js, range(6), right, jsems)
    for copy in lefts + rights:
        copy.start()
    for copy in lefts:
        copy.wait()
    for i in range(2):
        fill_all(left.reshape(CUTS, 2 * PARTIAL, LANES), i, held.at[i])
    for copy in rights:
        copy.wait()


def begin(je, jf, _, held, total, now, later, right, jsems):
    rights = fetch_rights([je, jf], (6, 7), right, jsems)
    for copy in rights:
        copy.start()
    for copy in rights:
        copy.wait()
    source = right.reshape(CUTS, 4 * PARTIAL, LANES)
    fill_right(source, 0, now)
    for i in range(2):
        total[i] = dot(held[i], now[...])
    fill_right(source, PARTIAL, later)


def scatter(out, side, stages, sums, sems):
    base = 2 * ((lax.axis_index("col") % 2 + side) % 2)
    flat_stages = [s.reshape(CUTS, 2 * WIDTH, LANES) for s in stages]

    def flush(i, cut):
        return pltpu.make_async_copy(
            stages[i].at[cut], out.at[base + i, :, :, pl.ds(cut * LANES, LANES)], sems.at[i, cut]
        )

    def store(i, cut):
        for j in range(2):
            value = sums[i][:, pl.ds((cut * 2 + j) * LANES, LANES)]
            flat_stages[i][cut, pl.ds(j, WIDTH, stride=2), :] = value

    return flush, store


def end(fill, product, flush, store):
    fill(0)
    product(0)
    fill(1)
    product(1)
    for cut in range(CUTS):
        store(0, cut)
    for cut in range(CUTS):
        flush(0, cut).start()
    for cut in range(CUTS):
        store(1, cut)
        flush(1, cut).start()
    for i in range(2):
        for cut in range(CUTS):
            flush(i, cut).wait()


def finish_own(*refs):
    pieces, total, later = refs[:4], refs[4], refs[5]
    out, left, even, odd, sums, other_sums, stage, other_stage, isems, osems = refs[6:]
    held, sums, stages = (even, odd), (sums, other_sums), (stage, other_stage)
    flush, store = scatter(out, 0, stages, sums, osems)
    lefts = fetch_lefts(pieces, left, isems)
    for copy in lefts:
        copy.start()
    for copy in lefts:
        copy.wait()
    source = left.reshape(CUTS, 2 * PARTIAL, LANES)

    def fill(i):
        fill_all(source, i, held[i])

    def product(i):
        sums[i][...] = dot(held[i][...], later[...]) + total[i]

    end(fill, product, flush, store)


def finish_other(*refs):
    early, pieces, now, later = refs[:2], refs[2:6], refs[6], refs[7]
    out, left, even, odd, next_even, next_odd, sums, other_sums, stage, other_stage, isems, osems = refs[9:]
    held, late_held = (even, odd), (next_even, next_odd)
    sums, stages = (sums, other_sums), (stage, other_stage)
    flush, store = scatter(out, 1, stages, sums, osems)
    first = [early[n // 2].at[pl.ds(n % 2 * 2 * HALF, 2 * HALF)] for n in (0, 1, 3, 2)]
    lefts = [fetch_lefts(first, left.at[0], isems.at[0]), fetch_lefts(pieces, left.at[1], isems.at[1])]
    for copy in lefts[0] + lefts[1]:
        copy.start()
    for copy in lefts[0]:
        copy.wait()
    sources = [left.at[h].reshape(CUTS, 2 * PARTIAL, LANES) for h in range(2)]
    fill_all(sources[0], 0, held[0])
    for copy in lefts[1]:
        copy.wait()
    sums[0][...] = dot(held[0][...], now[...])
    fill_all(sources[1], 0, late_held[0])
    sums[0][...] += dot(late_held[0][...], later[...])
    fill_all(sources[0], 1, held[1])
    sums[1][...] = dot(held[1][...], now[...])
    fill_all(sources[1], 1, late_held[1])
    sums[1][...] += dot(late_held[1][...], later[...])
    for i in range(2):
        for cut in range(CUTS):
            store(i, cut)
            flush(i, cut).start()
    for i in range(2):
        for cut in range(CUTS):
            flush(i, cut).wait()


ANY = pl.BlockSpec(memory_space=pl.ANY)
NEAR = pl.BlockSpec(memory_space=pltpu.VMEM)
WIDE = 10 * LANES
HELD = pltpu.VMEM((WIDTH, DEPTH), jnp.bfloat16)
LEFT = pltpu.VMEM((CUTS, PARTIAL, 2, LANES), jnp.float32)
LEFT_SEMS = pltpu.SemaphoreType.DMA((CUTS, 2, GROUP))
PANEL = pltpu.VMEM((DEPTH, WIDE), jnp.bfloat16)
SUMS = pltpu.VMEM((2, WIDTH, WIDE), jnp.float32)
HELDS = pltpu.VMEM((2, WIDTH, DEPTH), jnp.bfloat16)
RIGHT = pltpu.VMEM((CUTS, 2 * PARTIAL, 2, LANES), jnp.float32)
SUM = pltpu.VMEM((WIDTH, WIDE), jnp.float32)
STAGE = pltpu.VMEM((CUTS, WIDTH, 2, LANES), jnp.float32)
LIMIT = 28 * 1024 * 1024
COST = pl.CostEstimate(flops=10**6, bytes_accessed=10**5, transcendentals=0)


def near(value):
    return pltpu.with_memory_space_constraint(value, pltpu.VMEM)


def call(kernel, args, kinds, shapes, scratch, aliases=None):
    nears = [near(arg) if kind is NEAR else arg for arg, kind in zip(args, kinds)]
    outs = [NEAR if isinstance(shape, type(SUMS)) else ANY for shape in shapes]
    return pl.pallas_call(
        kernel,
        out_shape=tuple(shapes),
        in_specs=kinds,
        out_specs=tuple(outs),
        scratch_shapes=scratch,
        input_output_aliases=aliases or {},
        compiler_params=pltpu.CompilerParams(vmem_limit_bytes=LIMIT),
        cost_estimate=COST,
    )(*nears)


def prepare_call(js, mine):
    scratch = [LEFT, pltpu.SemaphoreType.DMA((CUTS, 2, 6)), LEFT_SEMS]
    return call(prepare, [*js, *mine], [ANY] * 10, [RIGHT, HELDS], scratch)


def begin_call(js, right, held):
    scratch = [pltpu.SemaphoreType.DMA((CUTS, 2, 2))]
    args = [*js, right, held]
    return call(begin, args, [ANY] * 2 + [NEAR] * 2, [SUMS, PANEL, PANEL, RIGHT], scratch, {2: 3})[:3]


OUT = jax.ShapeDtypeStruct((4, WIDTH, 2, WIDTH), jnp.float32)
OUT_SEMS = pltpu.SemaphoreType.DMA((2, CUTS))


def own_call(pieces, total, later):
    scratch = [LEFT, HELD, HELD, SUM, SUM, STAGE, STAGE, LEFT_SEMS, OUT_SEMS]
    return call(finish_own, [*pieces, total, later], [ANY] * 4 + [NEAR] * 2, [OUT], scratch)[0]


def other_call(early, pieces, now, later, out):
    scratch = [
        pltpu.VMEM((2, CUTS, PARTIAL, 2, LANES), jnp.float32),
        HELD, HELD, HELD, HELD, SUM, SUM, STAGE, STAGE,
        pltpu.SemaphoreType.DMA((2, CUTS, 2, GROUP)),
        OUT_SEMS,
    ]
    args = [*early, *pieces, now, later, out]
    return call(finish_other, args, [ANY] * 6 + [NEAR] * 2 + [ANY], [OUT], scratch, {8: 0})[0]


def shards(amplitude, coupling):
    amps = jnp.transpose(amplitude, (1, 2, 0, 3)).reshape(HALF, 2, WIDTH)
    ints = coupling.reshape(HALF, 2, WIDTH)
    block = jnp.concatenate([ints, amps], axis=0)

    def way(core):
        return 1 - 2 * core

    def right(x, z, y, low, core):
        return x + way(core), z, y, low, core

    def left(x, z, y, low, core):
        return x - way(core), z, y, low, core

    def up(x, z, y, low, core):
        return x, z, y + way(core), low, core

    def down(x, z, y, low, core):
        return x, z, y - way(core), low, core

    def beyond(x, z, y, low, core):
        return x, z, y, low + 1, core

    def tilt(value, shift):
        return permute(value, lambda x, z, y, low, core: (x, low, y - x + shift, z + shift // 2, core))

    def mirror(value, shift):
        return permute(
            value, lambda x, z, y, low, core: (y + x - shift, z, y, low, core)
        )

    def swap(value):
        return permute(value, lambda x, z, y, low, core: (x, z, y, low, core + 1))

    amps, ints, block = together(amps, ints, block)
    far = permute(block, lambda x, z, y, low, core: (x, z + 1, y, low, core))
    ta = tilt(amps, 0)
    tw = tilt(ints, 2)
    ja = permute(block, right)
    jb = permute(block, left)
    ta, tw = together(ta, tw)
    ma = mirror(ta, 0)
    mw = mirror(tw, 2)

    ma, mw, ja, jb, far = together(ma, mw, ja, jb, far)
    held = jnp.concatenate([ma, mw], axis=0)
    a = permute(held, up)
    b = permute(held, down)
    beside = permute(held, beyond)
    jc = permute(far, right)
    jd = permute(far, left)
    e = permute(a, up)

    ja, jc, jd, beside, b = together(ja, jc, jd, beside, b)
    je = permute(ja, right)
    jf = permute(jd, left)
    panel, helds = prepare_call([block, far, ja, jb, jc, jd], [held, beside, a, b])
    e, beside, panel, helds = together(e, beside, panel, helds)
    f = permute(e, beyond)
    c = permute(beside, up)
    d = permute(beside, down)

    own, now, later = begin_call([je, jf], panel, helds)
    held, beside, a, b, e, c, d, f, own = together(held, beside, a, b, e, c, d, f, own)
    early = [swap(jnp.concatenate([held, beside], axis=0)), swap(jnp.concatenate([a, b], axis=0))]
    late = [swap(v) for v in (d, c, e, f)]
    out = own_call([c, d, e, f], own, later)
    return other_call(early, late, now, later, out)


def solution(mesh):
    placed = (P("col", "row", None, None), P("row", None, "col", None))
    return jax.shard_map(
        shards, mesh=mesh, in_specs=placed, out_specs=P("row", None, "col", None), check_vma=False
    )
```
